32 devices in a mesh: group: 8 (over y, x, core), blk: 4 (over z).
Axes of the slice: x: 2, y: 2, z: 4, core: 2. Of those that a mesh axis runs over, the one named last changes fastest.
Arguments:
- queries: bfloat16 [8192, 1024], P(('group', 'blk')), may hold values from -6 to 6
- keys: bfloat16 [8192, 1024], P(('group', 'blk')), may hold values from -6 to 6
- values: bfloat16 [8192, 1024], P(('group', 'blk')), may hold values from -6 to 6
- out_grad: bfloat16 [8192, 1024], P(('group', 'blk')), may hold values from -6 to 6
- send_rows: int32 [32, 32, 16], P(('group', 'blk')), may hold values from 0 to 256, as said below
- recv_slots: int32 [32, 256], P(('group', 'blk')), may hold values from 0 to 511, as said below
- scene_frames: int32 [8, 4], P('group', 'blk'), may hold values from 0 to 1, never falling along the last dimension, each value on 1 to 3 neighbouring positions
Outputs:
- query_grad: bfloat16 [8192, 1024], P(('group', 'blk'))
- key_grad: bfloat16 [8192, 1024], P(('group', 'blk'))
- value_grad: bfloat16 [8192, 1024], P(('group', 'blk'))
The draws below stay inside these ranges and needn't reach their ends.
Inputs may be any that keep to these rules, and one draw needn't show every extreme that they name: `send_rows`: entry [s, e, c] is a row of device s that goes to slot c of its message to device e, or 256 for an empty slot. Every row of every device is named exactly once; each message carries a run of consecutive rows of its source, in order, and the messages of one source follow one another in order of target; filled slots come first in each message; each message holds 0, 8 or 16 rows, some exactly 16; every device receives exactly 256 rows in all. `recv_slots`: row j of device e takes received slot s * 16 + c (message of device s, slot c), which is filled; each filled slot is taken once, in order of source device and then of slot. `scene_frames`: scene numbers never fall along a group's frames; each scene spans 1 to 3 frames.
All inputs are finite; a program needn't handle non-finite values.
Results may differ from the reference program's by a relative error of at most 0.012.
The reference program's roundings to bfloat16 on the way count: a program that leaves them out, or rounds other values in their place, can miss the bound.
Values may be sent and summed in bfloat16 or wider, within the bound.
A program may use at most 128 MiB of HBM per device.

```python
import math
import jax
import jax.numpy as jnp
import numpy as np
from jax import lax

HEADS = 16
HEAD_DIM = 64
D = 1024
TOK_DEV = 256
FRAME_TOK = 256
TOKENS = 8192
FRAMES_GROUP = 4
SCENES = 2
MOST_FRAMES = 3
N_GROUP = 8
N_BLK = 4


def plan_tables(key):
    devices = N_GROUP * N_BLK
    part_rows = TOK_DEV // devices
    capacity = 2 * part_rows
    order_key, offset_key = jax.random.split(key, 2)
    shuffled = jax.random.permutation(order_key, devices).astype(jnp.int32)
    offset_step = jax.random.randint(offset_key, (), 1, devices).astype(jnp.int32)
    source = jnp.arange(devices, dtype=jnp.int32)
    added_to = shuffled[source]
    taken_from = shuffled[(source + offset_step) % devices]
    columns = jnp.arange(devices, dtype=jnp.int32)[None, :]
    counts = part_rows + part_rows * (columns == added_to[:, None]).astype(jnp.int32) - part_rows * (columns == taken_from[:, None]).astype(jnp.int32)
    running_counts = jnp.cumsum(counts, axis=1).astype(jnp.int32)
    first_slot = running_counts - counts
    position = jnp.arange(TOK_DEV, dtype=jnp.int32)
    target = jnp.sum((running_counts[:, None, :] <= position[None, :, None]).astype(jnp.int32), axis=2).astype(jnp.int32)
    slot_index = position[None, :] - jnp.take_along_axis(first_slot, target, axis=1)
    row_orders = jnp.broadcast_to(position[None, :], (devices, TOK_DEV)).astype(jnp.int32)
    send_rows = jnp.full((devices, devices, capacity), TOK_DEV, jnp.int32).at[source[:, None], target, slot_index].set(row_orders)
    slot_all = jnp.arange(devices * capacity, dtype=jnp.int32)
    filled = (slot_all % capacity)[None, :] < counts.T[:, slot_all // capacity]
    sort_key = jnp.where(filled, 0, devices * capacity).astype(jnp.int32) + slot_all[None, :]
    recv_slots = jnp.argsort(sort_key, axis=1, stable=True)[:, :TOK_DEV].astype(jnp.int32)
    return (send_rows, recv_slots)


def draw_send_rows(key, part):
    return plan_tables(key)[0]


def draw_recv_slots(key, part):
    return plan_tables(key)[1]


def draw_queries(key, part):
    key = jax.random.fold_in(key, 11)
    key_normal = jax.random.fold_in(key, 0)
    drawn = jnp.clip(jax.random.normal(key_normal, (TOKENS, D), jnp.float32), -6.0, 6.0)
    return drawn.astype(jnp.bfloat16)


def draw_keys(key, part):
    key = jax.random.fold_in(key, 23)
    key_normal = jax.random.fold_in(key, 0)
    drawn = jnp.clip(jax.random.normal(key_normal, (TOKENS, D), jnp.float32), -6.0, 6.0)
    return drawn.astype(jnp.bfloat16)


def block_levels(stream_key, extent, shards, least, top_value):
    level = 1.0
    for dim, shards_of in shards:
        steps = jax.random.uniform(jax.random.fold_in(jax.random.fold_in(stream_key, 6), dim), (shards_of,), jnp.float32, least / len(shards), top_value / len(shards))
        level = level * jnp.repeat(jnp.exp(steps), extent[dim] // shards_of).reshape((-1,) + (1,) * (len(extent) - 1 - dim))
    return level


def split_up(count, total, limit, skew):
    loads = [(1 << 20) // math.isqrt(standing ** skew) + 1 for standing in range(2, count + 1)]
    spare, given = total - limit - (count - 1), [1] * (count - 1)
    while spare > 0:
        movable = [i for i in range(count - 1) if given[i] < limit]
        pool, remaining = sum([loads[i] for i in movable]), spare
        for i in movable:
            addition = min(limit - given[i], max(1, remaining * loads[i] // pool), spare)
            given[i] = given[i] + addition
            spare = spare - addition
    return np.array([limit] + given)


def ragged(own_key, count, total, bound, slope):
    if count == 2:
        one = jax.random.randint(own_key, (), max(1, total - bound), min(bound, total - 1) + 1)
        return jnp.stack([one, total - one])
    lengths = jnp.asarray(split_up(count, total, bound, slope), jnp.int32)
    pairs = (count - 1) // 2
    source_of, sink = lengths[1:1 + 2 * pairs:2], lengths[2:2 + 2 * pairs:2]
    room = jnp.minimum(source_of - 1, bound - sink)
    shifted = jax.random.randint(jax.random.fold_in(own_key, 1), (pairs,), 0, 1 << 20) % (room + 1)
    lengths = lengths.at[1:1 + 2 * pairs:2].set(source_of - shifted).at[2:2 + 2 * pairs:2].set(sink + shifted)
    return lengths[jax.random.permutation(jax.random.fold_in(own_key, 2), count)]


def scatter_about(key, dims, scale, reach, cuts=(), held_as=jnp.bfloat16):
    result = jax.random.normal(key, dims, jnp.float32) * scale
    if len(cuts) > 0:
        result = block_levels(key, dims, cuts, -0.22, 0.18) * result
    return jnp.clip(result, min=-reach, max=reach).astype(held_as)


def setup_inputs(seed: int = 0) -> dict:
    key_of = jax.random.split(jax.random.key(seed), 8)
    queries = draw_queries(jax.random.fold_in(key_of[7], 71), 0)
    keys = draw_keys(jax.random.fold_in(key_of[7], 71), 0)
    values = scatter_about(key_of[2], (TOKENS, D), 1.0, 6.0, ((0, 32),))
    out_grad = scatter_about(key_of[3], (TOKENS, D), 1.0, 6.0, ((0, 32),))
    send_rows = draw_send_rows(jax.random.fold_in(key_of[7], 71), 0)
    recv_slots = draw_recv_slots(jax.random.fold_in(key_of[7], 71), 0)
    scene_frames = jax.vmap(lambda own: jnp.searchsorted(jnp.cumsum(ragged(own, SCENES, FRAMES_GROUP, MOST_FRAMES, 2)), jnp.arange(FRAMES_GROUP), side="right"))(jax.random.split(key_of[6], N_GROUP)).reshape((N_GROUP, FRAMES_GROUP)).astype(jnp.int32)
    return dict(queries=queries, keys=keys, values=values, out_grad=out_grad, send_rows=send_rows, recv_slots=recv_slots, scene_frames=scene_frames)


LOW_SCORE = -1e30


def source_order(send_rows, recv_slots):
    capacity = send_rows.shape[2]
    source = (recv_slots // capacity).astype(jnp.int32)
    slot_index = (recv_slots % capacity).astype(jnp.int32)
    target = jnp.arange(recv_slots.shape[0], dtype=jnp.int32)[:, None]
    local_row = send_rows[source, target, slot_index]
    return (source * TOK_DEV + local_row).reshape(-1).astype(jnp.int32)


def group_backward(group_inputs):
    query_rows, key_rows, value_rows, grad_rows, scene_ids = group_inputs
    in_scene = scene_ids[:, None] == scene_ids[None, :]
    scale = HEAD_DIM ** -0.5

    def split_heads(array):
        return array.reshape(array.shape[0], HEADS, HEAD_DIM).transpose(1, 0, 2)

    def one_head(head_inputs):
        query_head, key_head, value_head, grad_head = head_inputs
        scores = jnp.where(in_scene, jnp.dot(query_head, key_head.T, preferred_element_type=jnp.float32) * scale, LOW_SCORE)
        row_max = jnp.max(scores, axis=1, keepdims=True)
        norm_sum = jnp.sum(jnp.where(in_scene, jnp.exp(scores - row_max), 0.0), axis=1, keepdims=True)
        log_norm = row_max + jnp.log(norm_sum)
        weights = jnp.where(in_scene, jnp.exp(scores - log_norm), 0.0)
        weight_grad = jnp.dot(grad_head, value_head.T, preferred_element_type=jnp.float32)
        row_dot = jnp.sum(weights * weight_grad, axis=1, keepdims=True)
        score_half = (weights * (weight_grad - row_dot) * scale).astype(jnp.bfloat16)
        weight_half = weights.astype(jnp.bfloat16)
        return (jnp.dot(score_half, key_head, preferred_element_type=jnp.float32),
                jnp.dot(score_half.T, query_head, preferred_element_type=jnp.float32),
                jnp.dot(weight_half.T, grad_head, preferred_element_type=jnp.float32))

    grads = lax.map(one_head, (split_heads(query_rows), split_heads(key_rows), split_heads(value_rows), split_heads(grad_rows)))
    return tuple(single.transpose(1, 0, 2).reshape(query_rows.shape[0], -1) for single in grads)


def reference(queries, keys, values, out_grad, send_rows, recv_slots, scene_frames):
    order = source_order(send_rows, recv_slots)
    group_length = N_BLK * TOK_DEV

    def regroup(array):
        return array[order].reshape(N_GROUP, group_length, array.shape[1])

    scene_ids = jnp.repeat(scene_frames, FRAME_TOK, axis=1)
    grads = lax.map(group_backward, (regroup(queries), regroup(keys), regroup(values), regroup(out_grad), scene_ids))

    def restore(array):
        flat = array.reshape(-1, array.shape[2]).astype(jnp.bfloat16)
        return jnp.zeros_like(flat).at[order].set(flat)

    return restore(grads[0]), restore(grads[1]), restore(grads[2])
```

```python
import functools

import jax
import jax.numpy as jnp
from jax import lax
from jax.experimental import pallas as pl
from jax.experimental.pallas import tpu as pltpu
from jax.sharding import PartitionSpec as P

HEAD_DIM = 64
PAIR = 2 * HEAD_DIM
MESH = pl.DeviceIdType.MESH
VMEM_LIMIT = 56 * 1024 * 1024


def turned(index, by, size):
    return lax.rem(index + by, size)


def greet(n_g, n_b, g, z):
    barrier = pltpu.get_barrier_semaphore()
    for i in range(1, n_b):
        pl.semaphore_signal(barrier, inc=1, device_id=(g, turned(z, i, n_b)), device_id_type=MESH)
    for i in range(1, n_g):
        pl.semaphore_signal(barrier, inc=1, device_id=(turned(g, i, n_g), z), device_id_type=MESH)
    pl.semaphore_wait(barrier, n_b + n_g - 2)


def remote(src, dst, send_sem, recv_sem, device):
    return pltpu.make_async_remote_copy(
        src_ref=src,
        dst_ref=dst,
        send_sem=send_sem,
        recv_sem=recv_sem,
        device_id=device,
        device_id_type=MESH,
    )


def send_hot(plan, rows, slots):
    named = plan[0:1, :slots]
    at = lax.broadcasted_iota(jnp.int32, (rows, slots), 0)
    return jnp.where(at == named, 1.0, 0.0).astype(jnp.float32)


def take_hot(plan, rows, dims, b):
    n_g, n_b, cap = dims
    taken = plan[1:2, :rows]
    if cap % 16 == 0:
        slot = lax.broadcasted_iota(jnp.int32, (n_g * n_b * cap, rows), 0)
    else:
        place = lax.broadcasted_iota(jnp.int32, (n_g * n_b * n_b * cap, rows), 0)
        slot = place // (n_b * cap) * cap + place % cap
        slot = jnp.where(place // cap % n_b == b, slot, -1)
    return jnp.where(slot == taken, 1.0, 0.0).astype(jnp.float32)


def regroup_kernel(
    dims, plan_ref, q, k, v, d, out_q, out_k, out_v, out_d, out_plan,
    plans, zbuf, sbuf, rbuf, pmat, umat,
    plan_s, plan_r, zs, zr, zl, gs, gr,
):
    n_g, n_b, cap = dims
    g, z = lax.axis_index("group"), lax.axis_index("blk")
    rows, width = zbuf.shape[2], zbuf.shape[3]
    slots = n_g * n_b * cap
    arrays = (q, k, v, d)
    outs = (out_q, out_k, out_v, out_d)
    greet(n_g, n_b, g, z)

    plan_sends = []
    for i in range(1, n_b):
        to = turned(z, i, n_b)
        copy = remote(plan_ref, plans.at[z], plan_s.at[to], plan_r.at[z], (g, to))
        copy.start()
        plan_sends.append(copy)

    def columns(index):
        return pl.ds(pl.multiple_of(index * width, width), width)

    z_sends, z_locals = [], []
    for a, array in enumerate(arrays):
        for i in range(1, n_b):
            to = turned(z, i, n_b)
            copy = remote(array.at[:, columns(to)], zbuf.at[a, z], zs.at[a, to], zr.at[a, z], (g, to))
            copy.start()
            z_sends.append(copy)
        local = pltpu.make_async_copy(array.at[:, columns(z)], zbuf.at[a, z], zl.at[a])
        local.start()
        z_locals.append(local)

    plans[z] = plan_ref[...]
    for i in range(1, n_b):
        source = turned(z, i, n_b)
        remote(plan_ref, plans.at[source], plan_s.at[source], plan_r.at[source], (g, source)).wait_recv()
    for b in range(n_b):
        plan = plans[b]
        out_plan[b] = plan
        pmat[b] = send_hot(plan, rows, slots).T.astype(jnp.bfloat16)
        umat[b] = take_hot(plan, rows, dims, b).T.astype(jnp.bfloat16)

    g_sends = []
    for a, array in enumerate(arrays):
        z_locals[a].wait()
        for i in range(1, n_b):
            source = turned(z, i, n_b)
            remote(
                array.at[:, columns(source)], zbuf.at[a, source], zs.at[a, source], zr.at[a, source], (g, source)
            ).wait_recv()
        for b in range(n_b):
            packed = jnp.dot(pmat[b], zbuf[a, b], preferred_element_type=jnp.float32)
            sbuf[a, :, b] = packed.astype(jnp.bfloat16).reshape(n_g, n_b * cap, width)
        for i in range(1, n_g):
            to = turned(g, i, n_g)
            copy = remote(sbuf.at[a, to], rbuf.at[a, g], gs.at[a, to], gr.at[a, g], (to, z))
            copy.start()
            g_sends.append(copy)
        rbuf[a, g] = sbuf[a, g]

    for a in range(len(arrays)):
        for i in range(1, n_g):
            source = turned(g, i, n_g)
            remote(
                sbuf.at[a, source], rbuf.at[a, source], gs.at[a, source], gr.at[a, source], (source, z)
            ).wait_recv()
        for b in range(n_b):
            if cap % 16 == 0:
                held = rbuf[a, :, :, b * cap : (b + 1) * cap]
            else:
                held = rbuf[a]
            held = held.reshape(-1, width)
            placed = jnp.dot(umat[b], held, preferred_element_type=jnp.float32)
            outs[a][b * rows : (b + 1) * rows, :] = placed.astype(jnp.bfloat16)

    for copy in plan_sends + z_sends + g_sends:
        copy.wait_send()


def restore_kernel(
    dims, plans, dq, dk, dv, out_q, out_k, out_v,
    sbuf, rbuf, zbuf, pmat, umat, gs, gr, zs, zr, zl,
):
    n_g, n_b, cap = dims
    g, z = lax.axis_index("group"), lax.axis_index("blk")
    rows, width = zbuf.shape[2], zbuf.shape[3]
    slots = n_g * n_b * cap
    arrays = (dq, dk, dv)
    outs = (out_q, out_k, out_v)
    greet(n_g, n_b, g, z)

    def columns(index):
        return pl.ds(pl.multiple_of(index * width, width), width)

    for b in range(n_b):
        umat[b] = take_hot(plans[b], rows, dims, b).astype(jnp.bfloat16)

    g_sends = []
    for a, array in enumerate(arrays):
        if cap % 16 == 0:
            for b in range(n_b):
                packed = jnp.dot(
                    umat[b], array[b * rows : (b + 1) * rows, :], preferred_element_type=jnp.float32
                )
                sbuf[a, :, :, b * cap : (b + 1) * cap] = packed.astype(jnp.bfloat16).reshape(
                    n_g, n_b, cap, width
                )
        else:
            packed = jnp.zeros((slots * n_b, width), jnp.float32)
            for b in range(n_b):
                packed += jnp.dot(
                    umat[b], array[b * rows : (b + 1) * rows, :], preferred_element_type=jnp.float32
                )
            sbuf[a] = packed.astype(jnp.bfloat16).reshape(n_g, n_b, n_b * cap, width)
        for i in range(1, n_g):
            to = turned(g, i, n_g)
            copy = remote(sbuf.at[a, to], rbuf.at[a, g], gs.at[a, to], gr.at[a, g], (to, z))
            copy.start()
            g_sends.append(copy)
        rbuf[a, g] = sbuf[a, g]

    for b in range(n_b):
        pmat[b] = send_hot(plans[b], rows, slots).astype(jnp.bfloat16)

    z_sends, z_locals = [], []
    for a in range(len(arrays)):
        for i in range(1, n_g):
            source = turned(g, i, n_g)
            remote(
                sbuf.at[a, source], rbuf.at[a, source], gs.at[a, source], gr.at[a, source], (source, z)
            ).wait_recv()
        for b in range(n_b):
            held = rbuf[a, :, b].reshape(slots, width)
            placed = jnp.dot(pmat[b], held, preferred_element_type=jnp.float32)
            zbuf[a, b] = placed.astype(jnp.bfloat16)
        for i in range(1, n_b):
            to = turned(z, i, n_b)
            copy = remote(zbuf.at[a, to], outs[a].at[:, columns(z)], zs.at[a, to], zr.at[a, z], (g, to))
            copy.start()
            z_sends.append(copy)
        local = pltpu.make_async_copy(zbuf.at[a, z], outs[a].at[:, columns(z)], zl.at[a])
        local.start()
        z_locals.append(local)

    for a in range(len(arrays)):
        z_locals[a].wait()
        for i in range(1, n_b):
            source = turned(z, i, n_b)
            remote(
                zbuf.at[a, source], outs[a].at[:, columns(source)], zs.at[a, source], zr.at[a, source], (g, source)
            ).wait_recv()
    for copy in g_sends + z_sends:
        copy.wait_send()


def dot_last(left, right):
    return lax.dot_general(left, right, (((1,), (1,)), ((), ())), preferred_element_type=jnp.float32)


def attend_kernel(n_b, scenes, q, k, v, d, dq, dk, dv, acc_k, acc_v):
    rows = q.shape[0] // n_b
    scale = HEAD_DIM ** (-0.5)
    acc_k[...] = jnp.zeros_like(acc_k)
    acc_v[...] = jnp.zeros_like(acc_v)
    lane = lax.broadcasted_iota(jnp.int32, (1, PAIR), 1)

    def of_head(array, head):
        inside = (lane >= head * HEAD_DIM) & (lane < (head + 1) * HEAD_DIM)
        return jnp.where(inside, array, jnp.zeros_like(array))

    def frame(i, first, count):
        at = pl.ds(pl.multiple_of(i * rows, rows), rows)
        near = pl.ds(pl.multiple_of(first * rows, rows), count * rows)
        q_rows, d_rows = q[at, :], d[at, :]
        k_rows, v_rows = k[near, :], v[near, :]
        k_turned = k_rows.T
        q_scaled = (q_rows.astype(jnp.float32) * scale).astype(jnp.bfloat16)
        turned_grads, add_k, add_v = [], None, None
        for head in range(2):
            d_head = of_head(d_rows, head)
            scores = dot_last(k_rows, of_head(q_scaled, head))
            weight_grad = dot_last(v_rows, d_head)
            weights = jnp.exp(scores - jnp.max(scores, axis=0, keepdims=True))
            inverse = 1.0 / jnp.sum(weights, axis=0, keepdims=True)
            weights = weights * inverse
            row_dot = jnp.sum(weights * weight_grad, axis=0, keepdims=True)
            score_half = (weights * (weight_grad - row_dot) * scale).astype(jnp.bfloat16)
            weight_half = weights.astype(jnp.bfloat16)
            turned_grads.append(
                jnp.dot(
                    k_turned[head * HEAD_DIM : (head + 1) * HEAD_DIM, :],
                    score_half,
                    preferred_element_type=jnp.float32,
                )
            )
            part_k = jnp.dot(score_half, of_head(q_rows, head), preferred_element_type=jnp.float32)
            part_v = jnp.dot(weight_half, d_head, preferred_element_type=jnp.float32)
            add_k = part_k if add_k is None else add_k + part_k
            add_v = part_v if add_v is None else add_v + part_v
        dq[at, :] = jnp.concatenate(turned_grads, axis=0).T.astype(jnp.bfloat16)
        acc_k[near, :] += add_k
        acc_v[near, :] += add_v

    def step(i, carry):
        mine = scenes[i]
        first, count = jnp.int32(0), jnp.int32(0)
        for j in range(n_b):
            first += jnp.where(scenes[j] < mine, 1, 0)
            count += jnp.where(scenes[j] == mine, 1, 0)
        for n in range(1, n_b):
            pl.when(count == n)(functools.partial(frame, i, first, n))
        return carry

    lax.fori_loop(0, n_b, step, 0)
    dk[...] = acc_k[...].astype(jnp.bfloat16)
    dv[...] = acc_v[...].astype(jnp.bfloat16)


def shards(n_g, n_b, queries, keys, values, out_grad, send_rows, recv_slots, scene_frames):
    rows, features = queries.shape
    cap = send_rows.shape[2]
    dims = (n_g, n_b, cap)
    slots = n_g * n_b * cap
    width = features // n_b
    long = max(slots, rows)
    plan = jnp.concatenate(
        [
            jnp.pad(send_rows.reshape(1, slots), ((0, 0), (0, long - slots))),
            jnp.pad(recv_slots, ((0, 0), (0, long - rows))),
            jnp.broadcast_to(scene_frames, (6, long)),
        ],
        axis=0,
    )
    in_vmem = pl.BlockSpec(memory_space=pltpu.VMEM)
    anywhere = pl.BlockSpec(memory_space=pl.ANY)
    group_rows = n_b * rows
    taken = slots if cap % 16 == 0 else slots * n_b
    half = jnp.bfloat16
    dma = pltpu.SemaphoreType.DMA
    *inbound, plans = pl.pallas_call(
        functools.partial(regroup_kernel, dims),
        out_shape=[jax.ShapeDtypeStruct((group_rows, width), half)] * 4
        + [jax.ShapeDtypeStruct((n_b, 8, long), jnp.int32)],
        in_specs=[in_vmem] + [anywhere] * 4,
        out_specs=[in_vmem] * 5,
        scratch_shapes=[
            pltpu.VMEM((n_b, 8, long), jnp.int32),
            pltpu.VMEM((4, n_b, rows, width), half),
            pltpu.VMEM((4, n_g, n_b, n_b * cap, width), half),
            pltpu.VMEM((4, n_g, n_b, n_b * cap, width), half),
            pltpu.VMEM((n_b, slots, rows), half),
            pltpu.VMEM((n_b, rows, taken), half),
            dma((n_b,)),
            dma((n_b,)),
            dma((4, n_b)),
            dma((4, n_b)),
            dma((4,)),
            dma((4, n_g)),
            dma((4, n_g)),
        ],
        compiler_params=pltpu.CompilerParams(
            collective_id=0, has_side_effects=True, vmem_limit_bytes=VMEM_LIMIT
        ),
        name="regroup",
    )(plan, queries, keys, values, out_grad)

    pair = pl.BlockSpec((group_rows, PAIR), lambda i, scenes: (0, i))
    grads = pl.pallas_call(
        functools.partial(attend_kernel, n_b),
        out_shape=[jax.ShapeDtypeStruct((group_rows, width), half)] * 3,
        grid_spec=pltpu.PrefetchScalarGridSpec(
            num_scalar_prefetch=1,
            grid=(width // PAIR,),
            in_specs=[pair] * 4,
            out_specs=[pair] * 3,
            scratch_shapes=[pltpu.VMEM((group_rows, PAIR), jnp.float32)] * 2,
        ),
        compiler_params=pltpu.CompilerParams(vmem_limit_bytes=VMEM_LIMIT),
        name="attend",
    )(plans[:, 2, 0], *inbound)

    return tuple(
        pl.pallas_call(
            functools.partial(restore_kernel, dims),
            out_shape=[jax.ShapeDtypeStruct((rows, features), half)] * 3,
            in_specs=[in_vmem] * 4,
            out_specs=[anywhere] * 3,
            scratch_shapes=[
                pltpu.VMEM((3, n_g, n_b, n_b * cap, width), half),
                pltpu.VMEM((3, n_g, n_b, n_b * cap, width), half),
                pltpu.VMEM((3, n_b, rows, width), half),
                pltpu.VMEM((n_b, rows, slots), half),
                pltpu.VMEM((n_b, taken, rows), half),
                dma((3, n_g)),
                dma((3, n_g)),
                dma((3, n_b)),
                dma((3, n_b)),
                dma((3,)),
            ],
            compiler_params=pltpu.CompilerParams(
                collective_id=1, has_side_effects=True, vmem_limit_bytes=VMEM_LIMIT
            ),
            name="restore",
        )(plans, *grads)
    )


def solution(mesh):
    both = P(("group", "blk"), None)
    placed = (both, both, both, both, P(("group", "blk"), None, None), both, P("group", "blk"))
    return jax.shard_map(
        functools.partial(shards, mesh.shape["group"], mesh.shape["blk"]),
        mesh=mesh,
        in_specs=placed,
        out_specs=(both, both, both),
        check_vma=False,
    )
```

```python
import functools

import jax
import jax.numpy as jnp
from jax import lax
from jax.experimental import pallas as pl
from jax.experimental.pallas import tpu as pltpu
from jax.sharding import PartitionSpec as P

HEAD_DIM = 64
PAIR = 2 * HEAD_DIM
MESH = pl.DeviceIdType.MESH
LOW_SCORE = -1e30
DEPTH = 3
VMEM_LIMIT = 56 * 1024 * 1024


def turned(index, by, size):
    return lax.rem(index + by, size)


def greet(n_g, n_b, g, z):
    barrier = pltpu.get_barrier_semaphore()
    for i in range(1, n_b):
        pl.semaphore_signal(barrier, inc=1, device_id=(g, turned(z, i, n_b)), device_id_type=MESH)
    for i in range(1, n_g):
        pl.semaphore_signal(barrier, inc=1, device_id=(turned(g, i, n_g), z), device_id_type=MESH)
    pl.semaphore_wait(barrier, n_b + n_g - 2)


def remote(src, dst, send_sem, recv_sem, device):
    return pltpu.make_async_remote_copy(
        src_ref=src,
        dst_ref=dst,
        send_sem=send_sem,
        recv_sem=recv_sem,
        device_id=device,
        device_id_type=MESH,
    )


def send_hot(plan, rows, slots):
    named = plan[0:1, :slots]
    at = lax.broadcasted_iota(jnp.int32, (rows, slots), 0)
    return jnp.where(at == named, 1.0, 0.0).astype(jnp.float32)


def take_hot(plan, rows, dims, b):
    n_g, n_b, cap = dims
    taken = plan[1:2, :rows]
    if cap % 16 == 0:
        slot = lax.broadcasted_iota(jnp.int32, (n_g * n_b * cap, rows), 0)
    else:
        place = lax.broadcasted_iota(jnp.int32, (n_g * n_b * n_b * cap, rows), 0)
        slot = place // (n_b * cap) * cap + place % cap
        slot = jnp.where(place // cap % n_b == b, slot, -1)
    return jnp.where(slot == taken, 1.0, 0.0).astype(jnp.float32)


def dot_first(left, right):
    return lax.dot_general(left, right, (((0,), (0,)), ((), ())), preferred_element_type=jnp.float32)


def dot_last(left, right):
    return lax.dot_general(left, right, (((1,), (1,)), ((), ())), preferred_element_type=jnp.float32)


def fused_kernel(
    dims, plan_ref, q, k, v, d, out_q, out_k, out_v,
    plans, zbuf, sbuf, rbuf, held, grads, back_s, back_r, back_z, acc_k, acc_v, pack, unpack, pack_t, unpack_t,
    plan_s, plan_r, zs, zr, zl, gs, gr, bgs, bgr, bzs, bzr, bzl,
):
    n_g, n_b, cap = dims
    g, z = lax.axis_index("group"), lax.axis_index("blk")
    rows = zbuf.shape[2]
    features = q.shape[1]
    width = features // n_b
    chunks = width // PAIR
    slots = n_g * n_b * cap
    aligned = cap % 16 == 0
    arrays = (q, k, v, d)
    outs = (out_q, out_k, out_v)
    steps = 4 * chunks
    scale = HEAD_DIM ** (-0.5)
    half = jnp.bfloat16
    z_others = [turned(z, i, n_b) for i in range(1, n_b)]
    g_others = [turned(g, i, n_g) for i in range(1, n_g)]
    sends = []

    def columns(index, chunk):
        return pl.ds(pl.multiple_of(index * width + chunk * PAIR, PAIR), PAIR)

    def go(copy):
        copy.start()
        sends.append(copy)

    def start_z(t):
        chunk, a = divmod(t, 4)
        for to in z_others:
            go(remote(arrays[a].at[:, columns(to, chunk)], zbuf.at[t, z], zs.at[t, to], zr.at[t, z], (g, to)))
        pltpu.make_async_copy(arrays[a].at[:, columns(z, chunk)], zbuf.at[t, z], zl.at[t]).start()

    def pack_step(t):
        chunk, a = divmod(t, 4)
        pltpu.make_async_copy(arrays[a].at[:, columns(z, chunk)], zbuf.at[t, z], zl.at[t]).wait()
        for other in z_others:
            remote(
                arrays[a].at[:, columns(other, chunk)],
                zbuf.at[t, other], zs.at[t, other], zr.at[t, other], (g, other),
            ).wait_recv()
        for b in range(n_b):
            packed = jnp.dot(pack[b], zbuf[t, b], preferred_element_type=jnp.float32)
            sbuf[t, :, b] = packed.astype(half).reshape(n_g, n_b * cap, PAIR)
        for to in g_others:
            go(remote(sbuf.at[t, to], rbuf.at[t, g], gs.at[t, to], gr.at[t, g], (to, z)))
        rbuf[t, g] = sbuf[t, g]

    def unpack_step(t):
        for other in g_others:
            remote(sbuf.at[t, other], rbuf.at[t, other], gs.at[t, other], gr.at[t, other], (other, z)).wait_recv()
        for b in range(n_b):
            if aligned:
                came = rbuf[t, :, :, b * cap : (b + 1) * cap].reshape(slots, PAIR)
                placed = jnp.dot(unpack[b], came, preferred_element_type=jnp.float32)
            else:
                placed = dot_first(unpack_t[b], rbuf[t].reshape(slots * n_b, PAIR))
            held[t, b * rows : (b + 1) * rows, :] = placed.astype(half)

    lane = lax.broadcasted_iota(jnp.int32, (1, PAIR), 1)

    def of_head(array, head):
        inside = (lane >= head * HEAD_DIM) & (lane < (head + 1) * HEAD_DIM)
        return jnp.where(inside, array, jnp.zeros_like(array))

    def attend(chunk, i):
        at = slice(i * rows, (i + 1) * rows)
        near = range(max(0, i - (n_b - 2)), min(n_b, i + n_b - 1))
        q_rows, d_rows = held[4 * chunk, at, :], held[4 * chunk + 3, at, :]
        q_scaled = (q_rows.astype(jnp.float32) * scale).astype(half)
        scene = plans[i, 2:3, :rows]
        same = {j: plans[j, 2:3, :rows] == scene for j in near}
        turned_grads = []
        add_k, add_v = {}, {}
        for head in range(2):
            d_head, q_head = of_head(d_rows, head), of_head(q_scaled, head)
            scores, weight_grad = {}, {}
            top = None
            for j in near:
                key_at = slice(j * rows, (j + 1) * rows)
                scores[j] = dot_last(held[4 * chunk + 1, key_at, :], q_head)
                weight_grad[j] = dot_last(held[4 * chunk + 2, key_at, :], d_head)
                high = jnp.where(same[j], jnp.max(scores[j], axis=0, keepdims=True), LOW_SCORE)
                top = high if top is None else jnp.maximum(top, high)
            total, dot = None, None
            weights = {}
            for j in near:
                weights[j] = jnp.exp(scores[j] - jnp.where(same[j], top, -LOW_SCORE))
                part = jnp.sum(weights[j], axis=0, keepdims=True)
                part_dot = jnp.sum(weights[j] * weight_grad[j], axis=0, keepdims=True)
                total = part if total is None else total + part
                dot = part_dot if dot is None else dot + part_dot
            inverse = 1.0 / total
            row_dot = dot * inverse
            turned_grad = None
            for j in near:
                key_at = slice(j * rows, (j + 1) * rows)
                normal = weights[j] * inverse
                score_half = (normal * (weight_grad[j] - row_dot)).astype(half)
                weight_half = normal.astype(half)
                key_t = held[4 * chunk + 1, key_at, :].T[head * HEAD_DIM : (head + 1) * HEAD_DIM, :]
                part = jnp.dot(key_t, score_half, preferred_element_type=jnp.float32)
                turned_grad = part if turned_grad is None else turned_grad + part
                part_k = jnp.dot(score_half, q_head, preferred_element_type=jnp.float32)
                part_v = jnp.dot(weight_half, d_head, preferred_element_type=jnp.float32)
                add_k[j] = part_k if head == 0 else add_k[j] + part_k
                add_v[j] = part_v if head == 0 else add_v[j] + part_v
            turned_grads.append(turned_grad * scale)
        for j in near:
            key_at = slice(j * rows, (j + 1) * rows)
            if i == max(0, j - (n_b - 2)):
                acc_k[key_at, :] = add_k[j]
                acc_v[key_at, :] = add_v[j]
            else:
                acc_k[key_at, :] += add_k[j]
                acc_v[key_at, :] += add_v[j]
        grads[3 * chunk, at, :] = jnp.concatenate(turned_grads, axis=0).T.astype(half)

    def back_pack(chunk, a):
        u = 3 * chunk + a
        if a == 1:
            grads[u] = acc_k[...].astype(half)
        if a == 2:
            grads[u] = acc_v[...].astype(half)
        if aligned:
            for b in range(n_b):
                packed = jnp.dot(
                    unpack_t[b], grads[u, b * rows : (b + 1) * rows, :], preferred_element_type=jnp.float32
                )
                back_s[u, :, :, b * cap : (b + 1) * cap] = packed.astype(half).reshape(n_g, n_b, cap, PAIR)
        else:
            packed = jnp.zeros((slots * n_b, PAIR), jnp.float32)
            for b in range(n_b):
                packed += jnp.dot(
                    unpack_t[b], grads[u, b * rows : (b + 1) * rows, :], preferred_element_type=jnp.float32
                )
            back_s[u] = packed.astype(half).reshape(n_g, n_b, n_b * cap, PAIR)
        for to in g_others:
            go(remote(back_s.at[u, to], back_r.at[u, g], bgs.at[u, to], bgr.at[u, g], (to, z)))
        back_r[u, g] = back_s[u, g]

    def back_middle(chunk, a):
        u = 3 * chunk + a
        for other in g_others:
            remote(
                back_s.at[u, other], back_r.at[u, other], bgs.at[u, other], bgr.at[u, other], (other, z)
            ).wait_recv()
        for b in range(n_b):
            came = back_r[u, :, b].reshape(slots, PAIR)
            back_z[u, b] = jnp.dot(pack_t[b], came, preferred_element_type=jnp.float32).astype(half)
        for to in z_others:
            go(remote(back_z.at[u, to], outs[a].at[:, columns(z, chunk)], bzs.at[u, to], bzr.at[u, z], (g, to)))
        pltpu.make_async_copy(back_z.at[u, z], outs[a].at[:, columns(z, chunk)], bzl.at[u]).start()

    def back_end(chunk, a):
        u = 3 * chunk + a
        pltpu.make_async_copy(back_z.at[u, z], outs[a].at[:, columns(z, chunk)], bzl.at[u]).wait()
        for other in z_others:
            remote(
                back_z.at[u, other],
                outs[a].at[:, columns(other, chunk)], bzs.at[u, other], bzr.at[u, other], (g, other),
            ).wait_recv()

    greet(n_g, n_b, g, z)
    for to in z_others:
        go(remote(plan_ref, plans.at[z], plan_s.at[to], plan_r.at[z], (g, to)))
    for t in range(min(DEPTH, steps)):
        start_z(t)
    plans[z] = plan_ref[...]
    for other in z_others:
        remote(plan_ref, plans.at[other], plan_s.at[other], plan_r.at[other], (g, other)).wait_recv()
    for b in range(n_b):
        hot = send_hot(plans[b], rows, slots)
        pack_t[b] = hot.astype(half)
        pack[b] = hot.T.astype(half)
        hot = take_hot(plans[b], rows, dims, b)
        unpack_t[b] = hot.astype(half)
        if aligned:
            unpack[b] = hot.T.astype(half)

    for t in range(steps):
        chunk, a = divmod(t, 4)
        if t + DEPTH < steps:
            start_z(t + DEPTH)
        pack_step(t)
        if t > 0:
            unpack_step(t - 1)
        if chunk > 0:
            for i in range(a * n_b // 4, (a + 1) * n_b // 4):
                attend(chunk - 1, i)
            if a == 3:
                for b in range(3):
                    back_pack(chunk - 1, b)
    unpack_step(steps - 1)
    last = chunks - 1
    waiting = [(c, a) for c in range(last) for a in range(3)]
    for i in range(n_b):
        attend(last, i)
        if waiting:
            back_middle(*waiting.pop(0))
    for a in range(3):
        back_pack(last, a)
    waiting += [(last, a) for a in range(3)]
    for c, a in waiting:
        back_middle(c, a)
    for c in range(chunks):
        for a in range(3):
            back_end(c, a)
    for copy in sends:
        copy.wait_send()


def shards(n_g, n_b, queries, keys, values, out_grad, send_rows, recv_slots, scene_frames):
    rows, features = queries.shape
    cap = send_rows.shape[2]
    dims = (n_g, n_b, cap)
    slots = n_g * n_b * cap
    chunks = features // n_b // PAIR
    long = max(slots, rows)
    plan = jnp.concatenate(
        [
            jnp.pad(send_rows.reshape(1, slots), ((0, 0), (0, long - slots))),
            jnp.pad(recv_slots, ((0, 0), (0, long - rows))),
            jnp.broadcast_to(scene_frames, (6, long)),
        ],
        axis=0,
    )
    in_vmem = pl.BlockSpec(memory_space=pltpu.VMEM)
    anywhere = pl.BlockSpec(memory_space=pl.ANY)
    group_rows = n_b * rows
    aligned = cap % 16 == 0
    taken = slots if aligned else slots * n_b
    half = jnp.bfloat16
    dma = pltpu.SemaphoreType.DMA
    out, back = 4 * chunks, 3 * chunks
    return tuple(
        pl.pallas_call(
            functools.partial(fused_kernel, dims),
            out_shape=[jax.ShapeDtypeStruct((rows, features), half)] * 3,
            in_specs=[in_vmem] + [anywhere] * 4,
            out_specs=[anywhere] * 3,
            scratch_shapes=[
                pltpu.VMEM((n_b, 8, long), jnp.int32),
                pltpu.VMEM((out, n_b, rows, PAIR), half),
                pltpu.VMEM((out, n_g, n_b, n_b * cap, PAIR), half),
                pltpu.VMEM((out, n_g, n_b, n_b * cap, PAIR), half),
                pltpu.VMEM((out, group_rows, PAIR), half),
                pltpu.VMEM((back, group_rows, PAIR), half),
                pltpu.VMEM((back, n_g, n_b, n_b * cap, PAIR), half),
                pltpu.VMEM((back, n_g, n_b, n_b * cap, PAIR), half),
                pltpu.VMEM((back, n_b, rows, PAIR), half),
                pltpu.VMEM((group_rows, PAIR), jnp.float32),
                pltpu.VMEM((group_rows, PAIR), jnp.float32),
                pltpu.VMEM((n_b, slots, rows), half),
                pltpu.VMEM((n_b, rows, slots) if aligned else (1, 16, 128), half),
                pltpu.VMEM((n_b, rows, slots), half),
                pltpu.VMEM((n_b, taken, rows), half),
                dma((n_b,)),
                dma((n_b,)),
                dma((out, n_b)),
                dma((out, n_b)),
                dma((out,)),
                dma((out, n_g)),
                dma((out, n_g)),
                dma((back, n_g)),
                dma((back, n_g)),
                dma((back, n_b)),
                dma((back, n_b)),
                dma((back,)),
            ],
            compiler_params=pltpu.CompilerParams(
                collective_id=0, has_side_effects=True, vmem_limit_bytes=VMEM_LIMIT
            ),
            name="fused",
        )(plan, queries, keys, values, out_grad)
    )


def solution(mesh):
    both = P(("group", "blk"), None)
    placed = (both, both, both, both, P(("group", "blk"), None, None), both, P("group", "blk"))
    return jax.shard_map(
        functools.partial(shards, mesh.shape["group"], mesh.shape["blk"]),
        mesh=mesh,
        in_specs=placed,
        out_specs=(both, both, both),
        check_vma=False,
    )
```

```python
import functools

import jax
import jax.numpy as jnp
from jax import lax
from jax.experimental import pallas as pl
from jax.experimental.pallas import tpu as pltpu
from jax.sharding import PartitionSpec as P

HEAD_DIM = 64
PAIR = 2 * HEAD_DIM
MESH = pl.DeviceIdType.MESH
LOW_SCORE = -1e30
AHEAD = 1
VMEM_LIMIT = 56 * 1024 * 1024


def turned(index, by, size):
    return lax.rem(index + by, size)


def greet(n_g, n_b, g, z):
    barrier = pltpu.get_barrier_semaphore()
    for i in range(1, n_b):
        pl.semaphore_signal(barrier, inc=1, device_id=(g, turned(z, i, n_b)), device_id_type=MESH)
    for i in range(1, n_g):
        pl.semaphore_signal(barrier, inc=1, device_id=(turned(g, i, n_g), z), device_id_type=MESH)
    pl.semaphore_wait(barrier, n_b + n_g - 2)


def remote(src, dst, send_sem, recv_sem, device):
    return pltpu.make_async_remote_copy(
        src_ref=src,
        dst_ref=dst,
        send_sem=send_sem,
        recv_sem=recv_sem,
        device_id=device,
        device_id_type=MESH,
    )


def send_hot(plan, rows, slots):
    named = plan[0:1, :slots]
    at = lax.broadcasted_iota(jnp.int32, (rows, slots), 0)
    return jnp.where(at == named, 1.0, 0.0).astype(jnp.float32)


def take_hot(plan, rows, dims, b):
    n_g, n_b, cap = dims
    taken = plan[1:2, :rows]
    if cap % 16 == 0:
        slot = lax.broadcasted_iota(jnp.int32, (n_g * n_b * cap, rows), 0)
    else:
        place = lax.broadcasted_iota(jnp.int32, (n_g * n_b * n_b * cap, rows), 0)
        slot = place // (n_b * cap) * cap + place % cap
        slot = jnp.where(place // cap % n_b == b, slot, -1)
    return jnp.where(slot == taken, 1.0, 0.0).astype(jnp.float32)


def dot_first(left, right):
    return lax.dot_general(left, right, (((0,), (0,)), ((), ())), preferred_element_type=jnp.float32)


def dot_last(left, right):
    return lax.dot_general(left, right, (((1,), (1,)), ((), ())), preferred_element_type=jnp.float32)


def fused_kernel(
    dims, plan_ref, q, k, v, d, out_q, out_k, out_v,
    plans, zbuf, sbuf, rbuf, held, grads, back_s, back_r, back_z, acc_k, acc_v, pack, unpack, pack_t, unpack_t,
    plan_s, plan_r, zs, zr, zl, gs, gr, bgs, bgr, bzs, bzr, bzl,
):
    n_g, n_b, cap = dims
    g, z = lax.axis_index("group"), lax.axis_index("blk")
    rows = zbuf.shape[2]
    features = q.shape[1]
    width = features // n_b
    chunks = width // PAIR
    slots = n_g * n_b * cap
    aligned = cap % 16 == 0
    arrays = (q, k, v, d)
    outs = (out_q, out_k, out_v)
    steps = 4 * chunks
    scale = HEAD_DIM ** (-0.5)
    half = jnp.bfloat16
    z_others = [turned(z, i, n_b) for i in range(1, n_b)]
    g_others = [turned(g, i, n_g) for i in range(1, n_g)]
    sends = []

    def columns(index, chunk):
        return pl.ds(pl.multiple_of(index * width + chunk * PAIR, PAIR), PAIR)

    def go(copy):
        copy.start()
        sends.append(copy)

    def start_z(t):
        chunk, a = divmod(t, 4)
        for to in z_others:
            go(remote(arrays[a].at[:, columns(to, chunk)], zbuf.at[t, z], zs.at[t, to], zr.at[t, z], (g, to)))
        pltpu.make_async_copy(arrays[a].at[:, columns(z, chunk)], zbuf.at[t, z], zl.at[t]).start()

    def pack_step(t):
        chunk, a = divmod(t, 4)
        pltpu.make_async_copy(arrays[a].at[:, columns(z, chunk)], zbuf.at[t, z], zl.at[t]).wait()
        for other in z_others:
            remote(
                arrays[a].at[:, columns(other, chunk)],
                zbuf.at[t, other], zs.at[t, other], zr.at[t, other], (g, other),
            ).wait_recv()
        for b in range(n_b):
            packed = jnp.dot(pack[b], zbuf[t, b], preferred_element_type=jnp.float32)
            sbuf[t, :, b] = packed.astype(half).reshape(n_g, n_b * cap, PAIR)
        for to in g_others:
            go(remote(sbuf.at[t, to], rbuf.at[t, g], gs.at[t, to], gr.at[t, g], (to, z)))
        rbuf[t, g] = sbuf[t, g]

    def unpack_step(t):
        for other in g_others:
            remote(sbuf.at[t, other], rbuf.at[t, other], gs.at[t, other], gr.at[t, other], (other, z)).wait_recv()
        for b in range(n_b):
            if aligned:
                came = rbuf[t, :, :, b * cap : (b + 1) * cap].reshape(slots, PAIR)
                placed = jnp.dot(unpack[b], came, preferred_element_type=jnp.float32)
            else:
                placed = dot_first(unpack_t[b], rbuf[t].reshape(slots * n_b, PAIR))
            held[t, b * rows : (b + 1) * rows, :] = placed.astype(half)

    lane = lax.broadcasted_iota(jnp.int32, (1, PAIR), 1)

    def of_head(array, head):
        inside = (lane >= head * HEAD_DIM) & (lane < (head + 1) * HEAD_DIM)
        return jnp.where(inside, array, jnp.zeros_like(array))

    def attend(chunk, i):
        at = slice(i * rows, (i + 1) * rows)
        near = range(max(0, i - (n_b - 2)), min(n_b, i + n_b - 1))
        q_rows, d_rows = held[4 * chunk, at, :], held[4 * chunk + 3, at, :]
        q_scaled = (q_rows.astype(jnp.float32) * scale).astype(half)
        scene = plans[i, 2:3, :rows]
        same = {j: plans[j, 2:3, :rows] == scene for j in near}
        turned_grads = []
        add_k, add_v = {}, {}
        for head in range(2):
            d_head, q_head = of_head(d_rows, head), of_head(q_scaled, head)
            scores, weight_grad = {}, {}
            top = None
            for j in near:
                key_at = slice(j * rows, (j + 1) * rows)
                scores[j] = dot_last(held[4 * chunk + 1, key_at, :], q_head)
                weight_grad[j] = dot_last(held[4 * chunk + 2, key_at, :], d_head)
                high = jnp.where(same[j], jnp.max(scores[j], axis=0, keepdims=True), LOW_SCORE)
                top = high if top is None else jnp.maximum(top, high)
            total, dot = None, None
            weights = {}
            for j in near:
                weights[j] = jnp.exp(scores[j] - jnp.where(same[j], top, -LOW_SCORE))
                part = jnp.sum(weights[j], axis=0, keepdims=True)
                part_dot = jnp.sum(weights[j] * weight_grad[j], axis=0, keepdims=True)
                total = part if total is None else total + part
                dot = part_dot if dot is None else dot + part_dot
            inverse = 1.0 / total
            row_dot = dot * inverse
            turned_grad = None
            for j in near:
                key_at = slice(j * rows, (j + 1) * rows)
                normal = weights[j] * inverse
                score_half = (normal * (weight_grad[j] - row_dot)).astype(half)
                weight_half = normal.astype(half)
                key_t = held[4 * chunk + 1, key_at, :].T[head * HEAD_DIM : (head + 1) * HEAD_DIM, :]
                part = jnp.dot(key_t, score_half, preferred_element_type=jnp.float32)
                turned_grad = part if turned_grad is None else turned_grad + part
                part_k = jnp.dot(score_half, q_head, preferred_element_type=jnp.float32)
                part_v = jnp.dot(weight_half, d_head, preferred_element_type=jnp.float32)
                add_k[j] = part_k if head == 0 else add_k[j] + part_k
                add_v[j] = part_v if head == 0 else add_v[j] + part_v
            turned_grads.append(turned_grad * scale)
        for j in near:
            key_at = slice(j * rows, (j + 1) * rows)
            if i == max(0, j - (n_b - 2)):
                acc_k[key_at, :] = add_k[j]
                acc_v[key_at, :] = add_v[j]
            else:
                acc_k[key_at, :] += add_k[j]
                acc_v[key_at, :] += add_v[j]
        grads[3 * chunk, at, :] = jnp.concatenate(turned_grads, axis=0).T.astype(half)

    def back_pack(chunk, a):
        u = 3 * chunk + a
        if aligned:
            for b in range(n_b):
                packed = jnp.dot(
                    unpack_t[b], grads[u, b * rows : (b + 1) * rows, :], preferred_element_type=jnp.float32
                )
                back_s[u, :, :, b * cap : (b + 1) * cap] = packed.astype(half).reshape(n_g, n_b, cap, PAIR)
        else:
            packed = jnp.zeros((slots * n_b, PAIR), jnp.float32)
            for b in range(n_b):
                packed += jnp.dot(
                    unpack_t[b], grads[u, b * rows : (b + 1) * rows, :], preferred_element_type=jnp.float32
                )
            back_s[u] = packed.astype(half).reshape(n_g, n_b, n_b * cap, PAIR)
        for to in g_others:
            go(remote(back_s.at[u, to], back_r.at[u, g], bgs.at[u, to], bgr.at[u, g], (to, z)))
        back_r[u, g] = back_s[u, g]
        if a == 0:
            grads[u + 1] = acc_k[...].astype(half)
            grads[u + 2] = acc_v[...].astype(half)

    def back_middle(chunk, a):
        u = 3 * chunk + a
        for other in g_others:
            remote(
                back_s.at[u, other], back_r.at[u, other], bgs.at[u, other], bgr.at[u, other], (other, z)
            ).wait_recv()
        for b in range(n_b):
            came = back_r[u, :, b].reshape(slots, PAIR)
            back_z[u, b] = jnp.dot(pack_t[b], came, preferred_element_type=jnp.float32).astype(half)
        for to in z_others:
            go(remote(back_z.at[u, to], outs[a].at[:, columns(z, chunk)], bzs.at[u, to], bzr.at[u, z], (g, to)))
        pltpu.make_async_copy(back_z.at[u, z], outs[a].at[:, columns(z, chunk)], bzl.at[u]).start()

    def back_end(chunk, a):
        u = 3 * chunk + a
        pltpu.make_async_copy(back_z.at[u, z], outs[a].at[:, columns(z, chunk)], bzl.at[u]).wait()
        for other in z_others:
            remote(
                back_z.at[u, other],
                outs[a].at[:, columns(other, chunk)], bzs.at[u, other], bzr.at[u, other], (g, other),
            ).wait_recv()

    def back_rest(chunk):
        back_pack(chunk, 1)
        back_middle(chunk, 0)
        back_pack(chunk, 2)
        back_middle(chunk, 1)
        back_middle(chunk, 2)

    greet(n_g, n_b, g, z)
    for to in z_others:
        go(remote(plan_ref, plans.at[z], plan_s.at[to], plan_r.at[z], (g, to)))
    for t in range(AHEAD):
        start_z(t)
    plans[z] = plan_ref[...]
    for other in z_others:
        remote(plan_ref, plans.at[other], plan_s.at[other], plan_r.at[other], (g, other)).wait_recv()
    for b in range(n_b):
        hot = send_hot(plans[b], rows, slots)
        pack_t[b] = hot.astype(half)
        pack[b] = hot.T.astype(half)
        hot = take_hot(plans[b], rows, dims, b)
        unpack_t[b] = hot.astype(half)
        if aligned:
            unpack[b] = hot.T.astype(half)

    last = chunks - 1
    for t in range(steps):
        chunk, a = divmod(t, 4)
        if t + AHEAD < steps:
            start_z(t + AHEAD)
        pack_step(t)
        if t > 0:
            unpack_step(t - 1)
        if chunk > 0:
            for i in range(a * n_b // 4, (a + 1) * n_b // 4):
                attend(chunk - 1, i)
            if a == 3:
                back_pack(chunk - 1, 0)
        if chunk > 1 and a == 0:
            back_rest(chunk - 2)
    unpack_step(steps - 1)
    if chunks > 1:
        back_pack(last - 1, 1)
        attend(last, 0)
        back_middle(last - 1, 0)
        back_pack(last - 1, 2)
        attend(last, 1)
        back_middle(last - 1, 1)
        for i in range(2, n_b):
            attend(last, i)
        back_pack(last, 0)
        back_middle(last - 1, 2)
    else:
        for i in range(n_b):
            attend(last, i)
        back_pack(last, 0)
    back_rest(last)
    for c in range(chunks):
        for a in range(3):
            back_end(c, a)
    for copy in sends:
        copy.wait_send()


def shards(n_g, n_b, queries, keys, values, out_grad, send_rows, recv_slots, scene_frames):
    rows, features = queries.shape
    cap = send_rows.shape[2]
    dims = (n_g, n_b, cap)
    slots = n_g * n_b * cap
    chunks = features // n_b // PAIR
    long = max(slots, rows)
    plan = jnp.concatenate(
        [
            jnp.pad(send_rows.reshape(1, slots), ((0, 0), (0, long - slots))),
            jnp.pad(recv_slots, ((0, 0), (0, long - rows))),
            jnp.broadcast_to(scene_frames, (6, long)),
        ],
        axis=0,
    )
    in_vmem = pl.BlockSpec(memory_space=pltpu.VMEM)
    anywhere = pl.BlockSpec(memory_space=pl.ANY)
    group_rows = n_b * rows
    aligned = cap % 16 == 0
    taken = slots if aligned else slots * n_b
    half = jnp.bfloat16
    dma = pltpu.SemaphoreType.DMA
    out, back = 4 * chunks, 3 * chunks
    return tuple(
        pl.pallas_call(
            functools.partial(fused_kernel, dims),
            out_shape=[jax.ShapeDtypeStruct((rows, features), half)] * 3,
            in_specs=[in_vmem] + [anywhere] * 4,
            out_specs=[anywhere] * 3,
            scratch_shapes=[
                pltpu.VMEM((n_b, 8, long), jnp.int32),
                pltpu.VMEM((out, n_b, rows, PAIR), half),
                pltpu.VMEM((out, n_g, n_b, n_b * cap, PAIR), half),
                pltpu.VMEM((out, n_g, n_b, n_b * cap, PAIR), half),
                pltpu.VMEM((out, group_rows, PAIR), half),
                pltpu.VMEM((back, group_rows, PAIR), half),
                pltpu.VMEM((back, n_g, n_b, n_b * cap, PAIR), half),
                pltpu.VMEM((back, n_g, n_b, n_b * cap, PAIR), half),
                pltpu.VMEM((back, n_b, rows, PAIR), half),
                pltpu.VMEM((group_rows, PAIR), jnp.float32),
                pltpu.VMEM((group_rows, PAIR), jnp.float32),
                pltpu.VMEM((n_b, slots, rows), half),
                pltpu.VMEM((n_b, rows, slots) if aligned else (1, 16, 128), half),
                pltpu.VMEM((n_b, rows, slots), half),
                pltpu.VMEM((n_b, taken, rows), half),
                dma((n_b,)),
                dma((n_b,)),
                dma((out, n_b)),
                dma((out, n_b)),
                dma((out,)),
                dma((out, n_g)),
                dma((out, n_g)),
                dma((back, n_g)),
                dma((back, n_g)),
                dma((back, n_b)),
                dma((back, n_b)),
                dma((back,)),
            ],
            compiler_params=pltpu.CompilerParams(
                collective_id=0, has_side_effects=True, vmem_limit_bytes=VMEM_LIMIT
            ),
            name="fused",
        )(plan, queries, keys, values, out_grad)
    )


def solution(mesh):
    both = P(("group", "blk"), None)
    placed = (both, both, both, both, P(("group", "blk"), None, None), both, P("group", "blk"))
    return jax.shard_map(
        functools.partial(shards, mesh.shape["group"], mesh.shape["blk"]),
        mesh=mesh,
        in_specs=placed,
        out_specs=(both, both, both),
        check_vma=False,
    )
```
